32 devices in a mesh: ctx: 8 (over z, x), head: 4 (over y, core).
Axes of the slice: x: 2, y: 2, z: 4, core: 2. Of those that a mesh axis runs over, the one named last changes fastest.
Arguments:
- queries: bfloat16 [512, 8192], P('ctx', 'head'), may hold values from -6 to 6
- keys: bfloat16 [512, 128], P('ctx'), may hold values from -6 to 6
- key_gain: float32 [128], replicated, may hold values from 0.25 to 1.75
- key_bias: float32 [128], replicated, may hold values from -0.5 to 0.5
- head_weights: bfloat16 [512, 64], P('ctx', 'head'), may hold values from -6 to 6
- positions: int32 [512], P('ctx'), may hold values from 0 to 383, as said below
Outputs:
- index_scores: float32 [512, 512], P(('ctx', 'head'))
The draws below stay inside these ranges and needn't reach their ends.
Inputs may be any that keep to these rules, and one draw needn't show every extreme that they name: `positions`: positions of packed documents: the first 384 tokens form one document and the rest is split into one to three documents at drawn points; a token's position counts from its document's first token.
All inputs are finite; a program needn't handle non-finite values.
Results may differ from the reference program's by a relative error of at most 0.0095.
Values may be sent and summed in bfloat16 or wider, within the bound.
A program may use at most 64 MiB of HBM per device.

```python
import math
import jax
import jax.numpy as jnp
import numpy as np
from jax import lax

H = 64
DH = 128
ROPE = 64
TOKENS = 512
N_HEAD = 4


def draw_positions(key, part):
    first_end = 3 * TOKENS // 4
    cuts = jax.random.randint(key, (2,), first_end + 1, TOKENS)
    token_ids = jnp.arange(TOKENS, dtype=jnp.int32)
    starts = jnp.where(token_ids >= first_end, first_end, 0).astype(jnp.int32)
    starts = jnp.where(token_ids >= cuts[0], jnp.maximum(starts, cuts[0]), starts)
    starts = jnp.where(token_ids >= cuts[1], jnp.maximum(starts, cuts[1]), starts)
    return (token_ids - starts).astype(jnp.int32)


def level_of(rng, dims, cuts, low, largest):
    def one(position, shards_of):
        steps = jax.random.uniform(jax.random.fold_in(jax.random.fold_in(rng, 6), position), (shards_of,), jnp.float32, low / len(cuts), largest / len(cuts))
        return jnp.repeat(jnp.exp(steps), dims[position] // shards_of).reshape((-1,) + (1,) * (len(dims) - position - 1))

    factor_of = one(*cuts[0])
    for cut in cuts[1:]:
        factor_of = factor_of * one(*cut)
    return factor_of


def normal_values(own_key, shape, scale, reach, split=(), kind=jnp.bfloat16):
    values = jax.random.normal(own_key, shape, jnp.float32) * scale
    if len(split) > 0:
        values = level_of(own_key, shape, split, -0.22, 0.18) * values
    return jnp.clip(values, min=-reach, max=reach).astype(kind)


def setup_inputs(seed: int = 0) -> dict:
    key_list = jax.random.split(jax.random.key(seed), 7)
    queries = normal_values(key_list[0], (TOKENS, H * DH), 1.0, 6.0, ((0, 8), (1, 4)))
    keys = normal_values(key_list[1], (TOKENS, DH), 1.0, 6.0, ((0, 8),))
    key_gain = jnp.clip(1.0 + 0.15 * jax.random.normal(key_list[2], (DH,), jnp.float32), 0.25, 1.75)
    key_bias = jnp.clip(jax.random.uniform(key_list[3], (DH,), jnp.float32, -0.5, 0.5), -0.5, 0.5)
    head_weights = normal_values(key_list[4], (TOKENS, H), 1.0, 6.0, ((0, 8), (1, 4)))
    positions = draw_positions(jax.random.fold_in(key_list[6], 71), 0)
    return {"queries": queries, "keys": keys, "key_gain": key_gain, "key_bias": key_bias, "head_weights": head_weights, "positions": positions}


def yarn_frequencies(rope_dims):
    half_dims = rope_dims // 2
    exponent = np.arange(0, rope_dims, 2) / rope_dims
    extra_freq = 1.0 / 10000.0 ** exponent
    inter_freq = extra_freq / 40.0

    def correction(beta):
        return rope_dims * math.log(4096.0 / (beta * 2.0 * math.pi)) / (2.0 * math.log(10000.0))
    low_dim = max(math.floor(correction(32.0)), 0)
    high_dim = min(math.ceil(correction(1.0)), rope_dims - 1)
    if high_dim == low_dim:
        high_dim = high_dim + 0.001
    ramp_values = np.clip((np.arange(half_dims) - low_dim) / (high_dim - low_dim), 0.0, 1.0)
    return (inter_freq * ramp_values + extra_freq * (1.0 - ramp_values)).astype(np.float32)

def rotate(values, angles):
    half_rope = ROPE // 2
    cosine = jnp.cos(angles)[:, None, :]
    sine = jnp.sin(angles)[:, None, :]
    first = values[..., :half_rope]
    second = values[..., half_rope:ROPE]
    return jnp.concatenate([first * cosine - second * sine, second * cosine + first * sine, values[..., ROPE:]], -1)

def key_norm(keys, key_gain, key_bias):
    values = keys.astype(jnp.float32)
    centered = values - lax.optimization_barrier(jnp.mean(values, axis=-1, keepdims=True))
    spread = lax.optimization_barrier(jnp.mean(centered * centered, axis=-1, keepdims=True))
    return centered * lax.rsqrt(spread + 1e-06) * key_gain + key_bias

def tile_scores(q_block, weights, k_block, groups, row_glob, row_doc, key_glob):
    rows_here = q_block.shape[0]
    heads_here = weights.shape[1]
    raw = lax.dot_general(q_block.reshape(rows_here * heads_here, DH), k_block, (((1,), (1,)), ((), ())), preferred_element_type=jnp.float32)
    active = jnp.maximum(raw, 0.0).reshape(rows_here, groups, heads_here // groups, k_block.shape[0])
    partial_sum = lax.optimization_barrier(jnp.sum(active * weights.reshape(rows_here, groups, heads_here // groups, 1), axis=2))
    visible = (key_glob[None, :] >= row_doc[:, None]) & (key_glob[None, :] <= row_glob[:, None])
    partial_sum = jnp.where(visible[:, None, :], partial_sum, jnp.zeros_like(partial_sum))
    return partial_sum.astype(jnp.bfloat16)

def reference(queries, keys, key_gain, key_bias, head_weights, positions):
    freqs = jnp.asarray(yarn_frequencies(ROPE))
    angles = positions.astype(jnp.float32)[:, None] * freqs[None, :]
    q_rot = rotate(queries.astype(jnp.float32).reshape(TOKENS, H, DH), angles).reshape(TOKENS, H * DH).astype(jnp.bfloat16)
    k_rot = rotate(key_norm(keys, key_gain, key_bias)[:, None, :], angles).reshape(TOKENS, DH).astype(jnp.bfloat16)
    weights = head_weights.astype(jnp.float32) * (1.0 / math.sqrt(H * DH))
    token_ids = jnp.arange(TOKENS, dtype=jnp.int32)
    doc_start = token_ids - positions
    block_len = math.gcd(TOKENS, 512)
    block_count = TOKENS // block_len

    def query_block(q_index):
        row_first = (q_index * block_len).astype(jnp.int32)
        q_block = lax.dynamic_slice_in_dim(q_rot, row_first, block_len, 0)
        w_block = lax.dynamic_slice_in_dim(weights, row_first, block_len, 0)
        row_glob = lax.dynamic_slice_in_dim(token_ids, row_first, block_len, 0)
        row_doc = lax.dynamic_slice_in_dim(doc_start, row_first, block_len, 0)

        def key_block(k_index):
            key_first = (k_index * block_len).astype(jnp.int32)
            k_block = lax.dynamic_slice_in_dim(k_rot, key_first, block_len, 0)
            key_glob = key_first + jnp.arange(block_len, dtype=jnp.int32)
            live = (key_first <= jnp.max(row_glob)) & (key_first + block_len > jnp.min(row_doc))

            def compute(operand):
                parts = tile_scores(q_block, w_block, k_block, N_HEAD, row_glob, row_doc, key_glob)
                return lax.optimization_barrier(jnp.sum(parts.astype(jnp.float32), axis=1))

            def skip(operand):
                return jnp.zeros((block_len, block_len), jnp.float32)
            return lax.cond(live, compute, skip, 0)
        tiles = lax.map(key_block, jnp.arange(block_count, dtype=jnp.int32))
        return jnp.transpose(tiles, (1, 0, 2)).reshape(block_len, TOKENS)
    result = lax.map(query_block, jnp.arange(block_count, dtype=jnp.int32))
    return result.reshape(TOKENS, TOKENS)
```

```python
import functools
import math

import jax
import jax.numpy as jnp
import numpy as np
from jax import lax
from jax.experimental import pallas as pl
from jax.experimental.pallas import tpu as pltpu
from jax.sharding import PartitionSpec as P

H = 64
DH = 128
ROPE = 64
MESH = pl.DeviceIdType.MESH


def yarn_frequencies(rope_dims):
    half_dims = rope_dims // 2
    exponent = np.arange(0, rope_dims, 2) / rope_dims
    extra_freq = 1.0 / 10000.0**exponent
    inter_freq = extra_freq / 40.0

    def correction(beta):
        return rope_dims * math.log(4096.0 / (beta * 2.0 * math.pi)) / (2.0 * math.log(10000.0))

    low_dim = max(math.floor(correction(32.0)), 0)
    high_dim = min(math.ceil(correction(1.0)), rope_dims - 1)
    ramp_values = np.clip((np.arange(half_dims) - low_dim) / (high_dim - low_dim), 0.0, 1.0)
    return (inter_freq * ramp_values + extra_freq * (1.0 - ramp_values)).astype(np.float32)


def sin_cos(angle):
    turns = jnp.floor(angle * (2.0 / math.pi) + 0.5)
    rest = angle - turns * 1.5703125
    rest = rest - turns * 4.837512969970703125e-4
    rest = rest - turns * 7.54978995489188216e-8
    square = rest * rest
    sine = ((-1.9515295891e-4 * square + 8.3321608736e-3) * square - 1.6666654611e-1) * (
        square * rest
    ) + rest
    cosine = (
        ((2.443315711809948e-5 * square - 1.388731625493765e-3) * square + 4.166664568298827e-2)
        * (square * square)
        - 0.5 * square
        + 1.0
    )
    quadrant = turns.astype(jnp.int32)
    odd = (quadrant & 1) == 1
    sine_out = jnp.where(odd, cosine, sine)
    cosine_out = jnp.where(odd, sine, cosine)
    sine_out = jnp.where((quadrant & 2) == 2, -sine_out, sine_out)
    cosine_out = jnp.where(((quadrant + 1) & 2) == 2, -cosine_out, cosine_out)
    return sine_out, cosine_out


def kernel(
    n_ctx,
    n_head,
    chunk,
    queries_hbm,
    keys_hbm,
    gain_hbm,
    bias_hbm,
    weights_hbm,
    positions_hbm,
    freq_hbm,
    out_ref,
    q_in,
    k_in,
    gain_in,
    bias_in,
    w_in,
    pos_in,
    freq_in,
    q_rot,
    w_wide,
    k_all,
    part_out,
    part_in,
    in_sem,
    key_send,
    key_recv,
    part_send,
    part_recv,
):
    c = lax.axis_index("ctx")
    g = lax.axis_index("head")
    rows = q_in.shape[0]
    heads = q_in.shape[1] // DH
    rows_each = rows // n_head
    tokens = n_ctx * rows
    first_end = 3 * tokens // 4
    late = c * rows >= first_end
    src_first = jnp.where(late, first_end // rows, 0)
    crossing = (c + 1) * rows > first_end
    dst_end = jnp.where(crossing, n_ctx, -(-first_end // rows))

    barrier = pltpu.get_barrier_semaphore()

    def greet(i, carry):
        pl.semaphore_signal(barrier, inc=1, device_id={"ctx": i, "head": g}, device_id_type=MESH)
        return carry

    lax.fori_loop(src_first, c, greet, 0)
    for d in range(1, n_head):
        pl.semaphore_signal(
            barrier,
            inc=1,
            device_id={"ctx": c, "head": lax.rem(g + d, n_head)},
            device_id_type=MESH,
        )

    copies = [
        pltpu.make_async_copy(src, dst, in_sem.at[i])
        for i, (src, dst) in enumerate(
            [
                (positions_hbm, pos_in),
                (freq_hbm, freq_in),
                (keys_hbm, k_in),
                (gain_hbm, gain_in),
                (bias_hbm, bias_in),
                (weights_hbm, w_in),
                (queries_hbm, q_in),
            ]
        )
    ]
    for copy in copies:
        copy.start()
    out_ref[...] = jnp.zeros_like(out_ref)

    copies[0].wait()
    copies[1].wait()
    pos_wide = jnp.broadcast_to(pos_in[...].reshape(1, rows).astype(jnp.float32), (rows, rows))
    here = lax.broadcasted_iota(jnp.int32, (rows, rows), 0)
    there = lax.broadcasted_iota(jnp.int32, (rows, rows), 1)
    pos = jnp.sum(jnp.where(here == there, pos_wide, 0.0), axis=1, keepdims=True)
    sine, cosine = sin_cos(pos * freq_in[...])
    lane = lax.broadcasted_iota(jnp.int32, (rows, DH), 1)
    half = ROPE // 2
    sine_low = jnp.where(lane < half, -sine, 0.0)
    sine_high = jnp.where((lane >= half) & (lane < ROPE), sine, 0.0)

    def rotate(values):
        return (
            values * cosine
            + pltpu.roll(values, DH - half, 1) * sine_low
            + pltpu.roll(values, half, 1) * sine_high
        )

    for copy in copies[2:5]:
        copy.wait()
    values = k_in[...].astype(jnp.float32)
    centered = values - jnp.mean(values, axis=-1, keepdims=True)
    spread = jnp.mean(centered * centered, axis=-1, keepdims=True)
    normed = centered * lax.rsqrt(spread + 1e-06) * gain_in[...].reshape(1, DH) + bias_in[
        ...
    ].reshape(1, DH)
    mine = pl.ds(pl.multiple_of(c * rows, rows), rows)
    k_all[mine, :] = rotate(normed).astype(jnp.bfloat16)

    pl.semaphore_wait(barrier, dst_end - c - 1 + n_head - 1)

    def key_copy(owner, target):
        place = pl.ds(pl.multiple_of(owner * rows, rows), rows)
        return pltpu.make_async_remote_copy(
            src_ref=k_all.at[place],
            dst_ref=k_all.at[place],
            send_sem=key_send.at[target],
            recv_sem=key_recv.at[owner],
            device_id={"ctx": target, "head": g},
            device_id_type=MESH,
        )

    def send_keys(i, carry):
        key_copy(c, dst_end + c - i).start()
        return carry

    lax.fori_loop(c + 1, dst_end, send_keys, 0)

    copies[5].wait()
    copies[6].wait()
    scale = 1.0 / math.sqrt(H * DH)
    for h in range(heads):
        q_rot[h * rows : (h + 1) * rows, :] = rotate(
            q_in[:, h * DH : (h + 1) * DH].astype(jnp.float32)
        ).astype(jnp.bfloat16)
        w_wide[h] = jnp.broadcast_to(w_in[:, h : h + 1].astype(jnp.float32) * scale, (rows, DH))

    row_glob = c * rows + lax.broadcasted_iota(jnp.int32, (rows, 1), 0)
    row_doc = row_glob - pos.astype(jnp.int32)
    per_chunk = chunk // rows
    chunk_first = src_first // per_chunk
    chunk_end = c // per_chunk + 1

    def part_copy(t, d):
        peer = lax.rem(g + d, n_head)
        return pltpu.make_async_remote_copy(
            src_ref=part_out.at[t, peer],
            dst_ref=part_in.at[t, d - 1],
            send_sem=part_send.at[t, d - 1],
            recv_sem=part_recv.at[t, d - 1],
            device_id={"ctx": c, "head": peer},
            device_id_type=MESH,
        )

    def score(t, carry):
        def arrive(i, carry):
            key_copy(i, c).wait_recv()
            return carry

        lax.fori_loop(
            jnp.maximum(src_first, t * per_chunk),
            jnp.minimum(c, (t + 1) * per_chunk),
            arrive,
            0,
        )
        first = pl.multiple_of(t * chunk, chunk)
        raw = lax.dot_general(
            q_rot[...],
            k_all[pl.ds(first, chunk), :],
            (((1,), (1,)), ((), ())),
            preferred_element_type=jnp.float32,
        )
        total = jnp.zeros((rows, chunk), jnp.float32)
        for h in range(heads):
            weight = w_wide[h]
            if chunk > DH:
                weight = jnp.concatenate([weight] * (chunk // DH), axis=1)
            total += jnp.maximum(raw[h * rows : (h + 1) * rows, :], 0.0) * weight
        key_glob = first + lax.broadcasted_iota(jnp.int32, (rows, chunk), 1)
        visible = (key_glob >= row_doc) & (key_glob <= row_glob)
        part = jnp.where(visible, total, 0.0).astype(jnp.bfloat16)
        for h in range(n_head):
            part_out[t, h] = part[h * rows_each : (h + 1) * rows_each, :]
        for d in range(1, n_head):
            part_copy(t, d).start()
        return carry

    lax.fori_loop(chunk_first, chunk_end, score, 0)

    def gather(t, carry):
        total = part_out[t, g].astype(jnp.float32)
        for d in range(1, n_head):
            part_copy(t, d).wait_recv()
            total += part_in[t, d - 1].astype(jnp.float32)
        out_ref[:, pl.ds(pl.multiple_of(t * chunk, chunk), chunk)] = total
        return carry

    lax.fori_loop(chunk_first, chunk_end, gather, 0)

    def sent_keys(i, carry):
        key_copy(c, i).wait_send()
        return carry

    lax.fori_loop(c + 1, dst_end, sent_keys, 0)

    def sent_parts(t, carry):
        for d in range(1, n_head):
            part_copy(t, d).wait_send()
        return carry

    lax.fori_loop(chunk_first, chunk_end, sent_parts, 0)


def solution(mesh):
    n_ctx, n_head = mesh.shape["ctx"], mesh.shape["head"]
    freqs = yarn_frequencies(ROPE)
    freq_wide = np.concatenate([freqs, freqs, np.zeros(DH - ROPE, np.float32)])[None, :]

    def on_device(queries, keys, key_gain, key_bias, head_weights, positions):
        rows = queries.shape[0]
        heads = queries.shape[1] // DH
        tokens = n_ctx * rows
        chunk = max(DH, tokens // 16)
        n_chunk = tokens // chunk
        rows_each = rows // n_head
        return pl.pallas_call(
            functools.partial(kernel, n_ctx, n_head, chunk),
            out_shape=jax.ShapeDtypeStruct((rows_each, tokens), jnp.float32),
            in_specs=[pl.BlockSpec(memory_space=pl.ANY)] * 7,
            out_specs=pl.BlockSpec(memory_space=pltpu.VMEM),
            scratch_shapes=[
                pltpu.VMEM(queries.shape, jnp.bfloat16),
                pltpu.VMEM(keys.shape, jnp.bfloat16),
                pltpu.VMEM(key_gain.shape, jnp.float32),
                pltpu.VMEM(key_bias.shape, jnp.float32),
                pltpu.VMEM(head_weights.shape, jnp.bfloat16),
                pltpu.VMEM(positions.shape, jnp.int32),
                pltpu.VMEM((1, DH), jnp.float32),
                pltpu.VMEM((heads * rows, DH), jnp.bfloat16),
                pltpu.VMEM((heads, rows, DH), jnp.float32),
                pltpu.VMEM((tokens, DH), jnp.bfloat16),
                pltpu.VMEM((n_chunk, n_head, rows_each, chunk), jnp.bfloat16),
                pltpu.VMEM((n_chunk, n_head - 1, rows_each, chunk), jnp.bfloat16),
                pltpu.SemaphoreType.DMA((7,)),
                pltpu.SemaphoreType.DMA((n_ctx,)),
                pltpu.SemaphoreType.DMA((n_ctx,)),
                pltpu.SemaphoreType.DMA((n_chunk, n_head - 1)),
                pltpu.SemaphoreType.DMA((n_chunk, n_head - 1)),
            ],
            compiler_params=pltpu.CompilerParams(
                collective_id=0, has_side_effects=True, vmem_limit_bytes=32 * 1024 * 1024
            ),
        )(queries, keys, key_gain, key_bias, head_weights, positions, jnp.asarray(freq_wide))

    in_specs = (P("ctx", "head"), P("ctx", None), P(), P(), P("ctx", "head"), P("ctx"))
    out_specs = P(("ctx", "head"), None)
    return jax.shard_map(
        on_device, mesh=mesh, in_specs=in_specs, out_specs=out_specs, check_vma=False
    )
```

```python
import functools
import math

import jax
import jax.numpy as jnp
import numpy as np
from jax import lax
from jax.experimental import pallas as pl
from jax.experimental.pallas import tpu as pltpu
from jax.sharding import PartitionSpec as P

H = 64
DH = 128
ROPE = 64
MESH = pl.DeviceIdType.MESH


def yarn_frequencies(rope_dims):
    half_dims = rope_dims // 2
    exponent = np.arange(0, rope_dims, 2) / rope_dims
    extra_freq = 1.0 / 10000.0**exponent
    inter_freq = extra_freq / 40.0

    def correction(beta):
        return rope_dims * math.log(4096.0 / (beta * 2.0 * math.pi)) / (2.0 * math.log(10000.0))

    low_dim = max(math.floor(correction(32.0)), 0)
    high_dim = min(math.ceil(correction(1.0)), rope_dims - 1)
    ramp_values = np.clip((np.arange(half_dims) - low_dim) / (high_dim - low_dim), 0.0, 1.0)
    return (inter_freq * ramp_values + extra_freq * (1.0 - ramp_values)).astype(np.float32)


def sin_cos(angle):
    turns = jnp.floor(angle * (2.0 / math.pi) + 0.5)
    rest = angle - turns * 1.5703125
    rest = rest - turns * 4.837512969970703125e-4
    rest = rest - turns * 7.54978995489188216e-8
    square = rest * rest
    sine = ((-1.9515295891e-4 * square + 8.3321608736e-3) * square - 1.6666654611e-1) * (
        square * rest
    ) + rest
    cosine = (
        ((2.443315711809948e-5 * square - 1.388731625493765e-3) * square + 4.166664568298827e-2)
        * (square * square)
        - 0.5 * square
        + 1.0
    )
    quadrant = turns.astype(jnp.int32)
    odd = (quadrant & 1) == 1
    sine_out = jnp.where(odd, cosine, sine)
    cosine_out = jnp.where(odd, sine, cosine)
    sine_out = jnp.where((quadrant & 2) == 2, -sine_out, sine_out)
    cosine_out = jnp.where(((quadrant + 1) & 2) == 2, -cosine_out, cosine_out)
    return sine_out, cosine_out


def kernel(
    n_ctx,
    n_head,
    chunk,
    queries_hbm,
    keys_hbm,
    gain_hbm,
    bias_hbm,
    weights_hbm,
    positions_hbm,
    freq_hbm,
    out_ref,
    q_in,
    k_in,
    gain_in,
    bias_in,
    w_in,
    pos_in,
    freq_in,
    q_rot,
    w_wide,
    k_all,
    part_out,
    part_in,
    in_sem,
    key_send,
    key_recv,
    part_send,
    part_recv,
):
    c = lax.axis_index("ctx")
    g = lax.axis_index("head")
    rows = q_in.shape[0]
    heads = q_in.shape[1] // DH
    rows_each = rows // n_head
    tokens = n_ctx * rows
    first_end = 3 * tokens // 4
    late = c * rows >= first_end
    src_first = jnp.where(late, first_end // rows, 0)
    crossing = (c + 1) * rows > first_end
    dst_end = jnp.where(crossing, n_ctx, -(-first_end // rows))

    barrier = pltpu.get_barrier_semaphore()

    def greet(i, carry):
        pl.semaphore_signal(barrier, inc=1, device_id={"ctx": i, "head": g}, device_id_type=MESH)
        return carry

    lax.fori_loop(src_first, c, greet, 0)
    for d in range(1, n_head):
        pl.semaphore_signal(
            barrier,
            inc=1,
            device_id={"ctx": c, "head": lax.rem(g + d, n_head)},
            device_id_type=MESH,
        )

    copies = [
        pltpu.make_async_copy(src, dst, in_sem.at[i])
        for i, (src, dst) in enumerate(
            [
                (positions_hbm, pos_in),
                (freq_hbm, freq_in),
                (keys_hbm, k_in),
                (gain_hbm, gain_in),
                (bias_hbm, bias_in),
                (weights_hbm, w_in),
                (queries_hbm, q_in),
            ]
        )
    ]
    for copy in copies:
        copy.start()
    out_ref[...] = jnp.zeros_like(out_ref)

    copies[0].wait()
    copies[1].wait()
    pos_wide = jnp.broadcast_to(pos_in[...].reshape(1, rows).astype(jnp.float32), (rows, rows))
    here = lax.broadcasted_iota(jnp.int32, (rows, rows), 0)
    there = lax.broadcasted_iota(jnp.int32, (rows, rows), 1)
    pos = jnp.sum(jnp.where(here == there, pos_wide, 0.0), axis=1, keepdims=True)
    sine, cosine = sin_cos(pos * freq_in[...])
    lane = lax.broadcasted_iota(jnp.int32, (rows, DH), 1)
    half = ROPE // 2
    sine_low = jnp.where(lane < half, -sine, 0.0)
    sine_high = jnp.where((lane >= half) & (lane < ROPE), sine, 0.0)

    def rotate(values):
        return (
            values * cosine
            + pltpu.roll(values, DH - half, 1) * sine_low
            + pltpu.roll(values, half, 1) * sine_high
        )

    for copy in copies[2:5]:
        copy.wait()
    values = k_in[...].astype(jnp.float32)
    centered = values - jnp.mean(values, axis=-1, keepdims=True)
    spread = jnp.mean(centered * centered, axis=-1, keepdims=True)
    normed = centered * lax.rsqrt(spread + 1e-06) * gain_in[...].reshape(1, DH) + bias_in[
        ...
    ].reshape(1, DH)
    mine = pl.ds(pl.multiple_of(c * rows, rows), rows)
    k_all[mine, :] = rotate(normed).astype(jnp.bfloat16)

    pl.semaphore_wait(barrier, dst_end - c - 1 + n_head - 1)

    def key_copy(owner, target):
        place = pl.ds(pl.multiple_of(owner * rows, rows), rows)
        return pltpu.make_async_remote_copy(
            src_ref=k_all.at[place],
            dst_ref=k_all.at[place],
            send_sem=key_send.at[target],
            recv_sem=key_recv.at[owner],
            device_id={"ctx": target, "head": g},
            device_id_type=MESH,
        )

    def send_keys(i, carry):
        key_copy(c, dst_end + c - i).start()
        return carry

    lax.fori_loop(c + 1, dst_end, send_keys, 0)

    copies[5].wait()
    copies[6].wait()
    scale = 1.0 / math.sqrt(H * DH)
    weights = scale * lax.dot_general(
        (here == there).astype(jnp.bfloat16),
        w_in[...],
        (((1,), (1,)), ((), ())),
        preferred_element_type=jnp.float32,
    )
    for h in range(heads):
        q_rot[h * rows : (h + 1) * rows, :] = rotate(
            q_in[:, h * DH : (h + 1) * DH].astype(jnp.float32)
        ).astype(jnp.bfloat16)
        w_wide[h] = jnp.broadcast_to(weights[:, h : h + 1], (rows, DH))

    row_glob = c * rows + lax.broadcasted_iota(jnp.int32, (rows, 1), 0)
    row_doc = row_glob - pos.astype(jnp.int32)
    per_chunk = chunk // rows
    chunk_first = src_first // per_chunk
    chunk_end = c // per_chunk + 1

    def part_copy(t, d):
        peer = lax.rem(g + d, n_head)
        return pltpu.make_async_remote_copy(
            src_ref=part_out.at[t, peer],
            dst_ref=part_in.at[t, d - 1],
            send_sem=part_send.at[t, d - 1],
            recv_sem=part_recv.at[t, d - 1],
            device_id={"ctx": c, "head": peer},
            device_id_type=MESH,
        )

    def score(i, carry):
        t = chunk_end + chunk_first - 1 - i

        def arrive(i, carry):
            key_copy(i, c).wait_recv()
            return carry

        lax.fori_loop(
            jnp.maximum(src_first, t * per_chunk),
            jnp.minimum(c, (t + 1) * per_chunk),
            arrive,
            0,
        )
        first = pl.multiple_of(t * chunk, chunk)
        raw = lax.dot_general(
            q_rot[...],
            k_all[pl.ds(first, chunk), :],
            (((1,), (1,)), ((), ())),
            preferred_element_type=jnp.float32,
        )
        total = jnp.zeros((rows, chunk), jnp.float32)
        for h in range(heads):
            weight = w_wide[h]
            if chunk > DH:
                weight = jnp.concatenate([weight] * (chunk // DH), axis=1)
            total += jnp.maximum(raw[h * rows : (h + 1) * rows, :], 0.0) * weight
        key_glob = first + lax.broadcasted_iota(jnp.int32, (rows, chunk), 1)
        visible = (key_glob >= row_doc) & (key_glob <= row_glob)
        part = jnp.where(visible, total, 0.0).astype(jnp.bfloat16)
        for h in range(n_head):
            part_out[t, h] = part[h * rows_each : (h + 1) * rows_each, :]
        for d in range(1, n_head):
            part_copy(t, d).start()
        return carry

    lax.fori_loop(chunk_first, chunk_end, score, 0)

    def gather(i, carry):
        t = chunk_end + chunk_first - 1 - i
        total = part_out[t, g].astype(jnp.float32)
        for d in range(1, n_head):
            part_copy(t, d).wait_recv()
            total += part_in[t, d - 1].astype(jnp.float32)
        out_ref[:, pl.ds(pl.multiple_of(t * chunk, chunk), chunk)] = total
        return carry

    lax.fori_loop(chunk_first, chunk_end, gather, 0)

    def sent_keys(i, carry):
        key_copy(c, i).wait_send()
        return carry

    lax.fori_loop(c + 1, dst_end, sent_keys, 0)

    def sent_parts(t, carry):
        for d in range(1, n_head):
            part_copy(t, d).wait_send()
        return carry

    lax.fori_loop(chunk_first, chunk_end, sent_parts, 0)


def solution(mesh):
    n_ctx, n_head = mesh.shape["ctx"], mesh.shape["head"]
    freqs = yarn_frequencies(ROPE)
    freq_wide = np.concatenate([freqs, freqs, np.zeros(DH - ROPE, np.float32)])[None, :]

    def on_device(queries, keys, key_gain, key_bias, head_weights, positions):
        rows = queries.shape[0]
        heads = queries.shape[1] // DH
        tokens = n_ctx * rows
        chunk = max(DH, tokens // 16)
        n_chunk = tokens // chunk
        rows_each = rows // n_head
        return pl.pallas_call(
            functools.partial(kernel, n_ctx, n_head, chunk),
            out_shape=jax.ShapeDtypeStruct((rows_each, tokens), jnp.float32),
            in_specs=[pl.BlockSpec(memory_space=pltpu.HBM)] * 7,
            out_specs=pl.BlockSpec(memory_space=pltpu.VMEM),
            scratch_shapes=[
                pltpu.VMEM(queries.shape, jnp.bfloat16),
                pltpu.VMEM(keys.shape, jnp.bfloat16),
                pltpu.VMEM(key_gain.shape, jnp.float32),
                pltpu.VMEM(key_bias.shape, jnp.float32),
                pltpu.VMEM(head_weights.shape[::-1], jnp.bfloat16),
                pltpu.VMEM(positions.shape, jnp.int32),
                pltpu.VMEM((1, DH), jnp.float32),
                pltpu.VMEM((heads * rows, DH), jnp.bfloat16),
                pltpu.VMEM((heads, rows, DH), jnp.float32),
                pltpu.VMEM((tokens, DH), jnp.bfloat16),
                pltpu.VMEM((n_chunk, n_head, rows_each, chunk), jnp.bfloat16),
                pltpu.VMEM((n_chunk, n_head - 1, rows_each, chunk), jnp.bfloat16),
                pltpu.SemaphoreType.DMA((7,)),
                pltpu.SemaphoreType.DMA((n_ctx,)),
                pltpu.SemaphoreType.DMA((n_ctx,)),
                pltpu.SemaphoreType.DMA((n_chunk, n_head - 1)),
                pltpu.SemaphoreType.DMA((n_chunk, n_head - 1)),
            ],
            compiler_params=pltpu.CompilerParams(
                collective_id=0, has_side_effects=True, vmem_limit_bytes=60 * 1024 * 1024
            ),
        )(queries, keys, key_gain, key_bias, head_weights.T, positions, jnp.asarray(freq_wide))

    in_specs = (P("ctx", "head"), P("ctx", None), P(), P(), P("ctx", "head"), P("ctx"))
    out_specs = P(("ctx", "head"), None)
    return jax.shard_map(
        on_device, mesh=mesh, in_specs=in_specs, out_specs=out_specs, check_vma=False
    )
```

```python
import functools
import math

import jax
import jax.numpy as jnp
import numpy as np
from jax import lax
from jax.experimental import pallas as pl
from jax.experimental.pallas import tpu as pltpu
from jax.sharding import PartitionSpec as P

H = 64
DH = 128
ROPE = 64
MESH = pl.DeviceIdType.MESH


def yarn_frequencies(rope_dims):
    half_dims = rope_dims // 2
    exponent = np.arange(0, rope_dims, 2) / rope_dims
    extra_freq = 1.0 / 10000.0**exponent
    inter_freq = extra_freq / 40.0

    def correction(beta):
        return rope_dims * math.log(4096.0 / (beta * 2.0 * math.pi)) / (2.0 * math.log(10000.0))

    low_dim = max(math.floor(correction(32.0)), 0)
    high_dim = min(math.ceil(correction(1.0)), rope_dims - 1)
    ramp_values = np.clip((np.arange(half_dims) - low_dim) / (high_dim - low_dim), 0.0, 1.0)
    return (inter_freq * ramp_values + extra_freq * (1.0 - ramp_values)).astype(np.float32)


def sin_cos(angle):
    turns = jnp.floor(angle * (2.0 / math.pi) + 0.5)
    rest = angle - turns * 1.5703125
    rest = rest - turns * 4.837512969970703125e-4
    rest = rest - turns * 7.54978995489188216e-8
    square = rest * rest
    sine = ((-1.9515295891e-4 * square + 8.3321608736e-3) * square - 1.6666654611e-1) * (
        square * rest
    ) + rest
    cosine = (
        ((2.443315711809948e-5 * square - 1.388731625493765e-3) * square + 4.166664568298827e-2)
        * (square * square)
        - 0.5 * square
        + 1.0
    )
    quadrant = turns.astype(jnp.int32)
    odd = (quadrant & 1) == 1
    sine_out = jnp.where(odd, cosine, sine)
    cosine_out = jnp.where(odd, sine, cosine)
    sine_out = jnp.where((quadrant & 2) == 2, -sine_out, sine_out)
    cosine_out = jnp.where(((quadrant + 1) & 2) == 2, -cosine_out, cosine_out)
    return sine_out, cosine_out


def kernel(
    n_ctx,
    n_head,
    chunk,
    queries_hbm,
    keys_hbm,
    gain_hbm,
    bias_hbm,
    weights_hbm,
    positions_hbm,
    freq_hbm,
    out_ref,
    q_in,
    k_in,
    gain_in,
    bias_in,
    w_in,
    pos_in,
    freq_in,
    q_rot,
    w_wide,
    k_all,
    part_out,
    part_in,
    in_sem,
    key_send,
    key_recv,
    part_send,
    part_recv,
):
    c = lax.axis_index("ctx")
    g = lax.axis_index("head")
    rows = q_in.shape[0]
    heads = q_in.shape[1] // DH
    rows_each = rows // n_head
    tokens = n_ctx * rows
    first_end = 3 * tokens // 4
    late = c * rows >= first_end
    src_first = jnp.where(late, first_end // rows, 0)
    crossing = (c + 1) * rows > first_end
    dst_end = jnp.where(crossing, n_ctx, -(-first_end // rows))

    barrier = pltpu.get_barrier_semaphore()

    def greet(i, carry):
        pl.semaphore_signal(barrier, inc=1, device_id={"ctx": i, "head": g}, device_id_type=MESH)
        return carry

    lax.fori_loop(src_first, c, greet, 0)
    for d in range(1, n_head):
        pl.semaphore_signal(
            barrier,
            inc=1,
            device_id={"ctx": c, "head": lax.rem(g + d, n_head)},
            device_id_type=MESH,
        )

    copies = [
        pltpu.make_async_copy(src, dst, in_sem.at[i])
        for i, (src, dst) in enumerate(
            [
                (positions_hbm, pos_in),
                (freq_hbm, freq_in),
                (keys_hbm, k_in),
                (gain_hbm, gain_in),
                (bias_hbm, bias_in),
                (weights_hbm, w_in),
                (queries_hbm, q_in),
            ]
        )
    ]
    for copy in copies:
        copy.start()
    out_ref[...] = jnp.zeros_like(out_ref)

    for copy in copies[:5]:
        copy.wait()
    pos_wide = jnp.broadcast_to(pos_in[...].reshape(1, rows).astype(jnp.float32), (rows, rows))
    here = lax.broadcasted_iota(jnp.int32, (rows, rows), 0)
    there = lax.broadcasted_iota(jnp.int32, (rows, rows), 1)
    pos = jnp.sum(jnp.where(here == there, pos_wide, 0.0), axis=1, keepdims=True)
    sine, cosine = sin_cos(pos * freq_in[...])
    lane = lax.broadcasted_iota(jnp.int32, (rows, DH), 1)
    half = ROPE // 2
    sine_low = jnp.where(lane < half, -sine, 0.0)
    sine_high = jnp.where((lane >= half) & (lane < ROPE), sine, 0.0)

    def rotate(values):
        return (
            values * cosine
            + pltpu.roll(values, DH - half, 1) * sine_low
            + pltpu.roll(values, half, 1) * sine_high
        )

    values = k_in[...].astype(jnp.float32)
    centered = values - jnp.mean(values, axis=-1, keepdims=True)
    spread = jnp.mean(centered * centered, axis=-1, keepdims=True)
    normed = centered * lax.rsqrt(spread + 1e-06) * gain_in[...].reshape(1, DH) + bias_in[
        ...
    ].reshape(1, DH)
    mine = pl.ds(pl.multiple_of(c * rows, rows), rows)
    k_all[mine, :] = rotate(normed).astype(jnp.bfloat16)

    pl.semaphore_wait(barrier, dst_end - c - 1 + n_head - 1)

    def key_copy(owner, target):
        place = pl.ds(pl.multiple_of(owner * rows, rows), rows)
        return pltpu.make_async_remote_copy(
            src_ref=k_all.at[place],
            dst_ref=k_all.at[place],
            send_sem=key_send.at[target],
            recv_sem=key_recv.at[owner],
            device_id={"ctx": target, "head": g},
            device_id_type=MESH,
        )

    def send_keys(i, carry):
        key_copy(c, dst_end + c - i).start()
        return carry

    lax.fori_loop(c + 1, dst_end, send_keys, 0)

    copies[5].wait()
    copies[6].wait()
    scale = 1.0 / math.sqrt(H * DH)
    weights = scale * lax.dot_general(
        (here == there).astype(jnp.bfloat16),
        w_in[...],
        (((1,), (1,)), ((), ())),
        preferred_element_type=jnp.float32,
    )
    for h in range(heads):
        q_rot[h * rows : (h + 1) * rows, :] = rotate(
            q_in[:, h * DH : (h + 1) * DH].astype(jnp.float32)
        ).astype(jnp.bfloat16)
        w_wide[h] = jnp.broadcast_to(weights[:, h : h + 1], (rows, DH))

    row_glob = c * rows + lax.broadcasted_iota(jnp.int32, (rows, 1), 0)
    row_doc = row_glob - pos.astype(jnp.int32)
    per_chunk = chunk // rows
    chunk_first = src_first // per_chunk
    chunk_end = c // per_chunk + 1

    def part_copy(t, d):
        peer = lax.rem(g + d, n_head)
        return pltpu.make_async_remote_copy(
            src_ref=part_out.at[t, peer],
            dst_ref=part_in.at[t, d - 1],
            send_sem=part_send.at[t, d - 1],
            recv_sem=part_recv.at[t, d - 1],
            device_id={"ctx": c, "head": peer},
            device_id_type=MESH,
        )

    def score(i, carry):
        t = chunk_end + chunk_first - 1 - i

        def arrive(i, carry):
            key_copy(i, c).wait_recv()
            return carry

        lax.fori_loop(
            jnp.maximum(src_first, t * per_chunk),
            jnp.minimum(c, (t + 1) * per_chunk),
            arrive,
            0,
        )
        first = pl.multiple_of(t * chunk, chunk)
        raw = lax.dot_general(
            q_rot[...],
            k_all[pl.ds(first, chunk), :],
            (((1,), (1,)), ((), ())),
            preferred_element_type=jnp.float32,
        )
        total = jnp.zeros((rows, chunk), jnp.float32)
        for h in range(heads):
            weight = w_wide[h]
            if chunk > DH:
                weight = jnp.concatenate([weight] * (chunk // DH), axis=1)
            total += jnp.maximum(raw[h * rows : (h + 1) * rows, :], 0.0) * weight
        key_glob = first + lax.broadcasted_iota(jnp.int32, (rows, chunk), 1)
        visible = (key_glob >= row_doc) & (key_glob <= row_glob)
        part = jnp.where(visible, total, 0.0).astype(jnp.bfloat16)
        for h in range(n_head):
            part_out[t, h] = part[h * rows_each : (h + 1) * rows_each, :]
        for d in range(1, n_head):
            part_copy(t, d).start()
        return carry

    lax.fori_loop(chunk_first, chunk_end, score, 0)

    def gather(i, carry):
        t = chunk_end + chunk_first - 1 - i
        total = part_out[t, g].astype(jnp.float32)
        for d in range(1, n_head):
            part_copy(t, d).wait_recv()
            total += part_in[t, d - 1].astype(jnp.float32)
        out_ref[:, pl.ds(pl.multiple_of(t * chunk, chunk), chunk)] = total
        return carry

    lax.fori_loop(chunk_first, chunk_end, gather, 0)

    def sent_keys(i, carry):
        key_copy(c, i).wait_send()
        return carry

    lax.fori_loop(c + 1, dst_end, sent_keys, 0)

    def sent_parts(t, carry):
        for d in range(1, n_head):
            part_copy(t, d).wait_send()
        return carry

    lax.fori_loop(chunk_first, chunk_end, sent_parts, 0)


def solution(mesh):
    n_ctx, n_head = mesh.shape["ctx"], mesh.shape["head"]
    freqs = yarn_frequencies(ROPE)
    freq_wide = np.concatenate([freqs, freqs, np.zeros(DH - ROPE, np.float32)])[None, :]

    def on_device(queries, keys, key_gain, key_bias, head_weights, positions):
        rows = queries.shape[0]
        heads = queries.shape[1] // DH
        tokens = n_ctx * rows
        chunk = max(DH, tokens // 16)
        n_chunk = tokens // chunk
        rows_each = rows // n_head
        operands = (
            queries,
            keys,
            key_gain,
            key_bias,
            head_weights.T,
            positions,
            jnp.asarray(freq_wide),
        )
        return pl.pallas_call(
            functools.partial(kernel, n_ctx, n_head, chunk),
            out_shape=jax.ShapeDtypeStruct((rows_each, tokens), jnp.float32),
            in_specs=[pl.BlockSpec(memory_space=pltpu.HBM)] * 7,
            out_specs=pl.BlockSpec(memory_space=pltpu.VMEM),
            scratch_shapes=[
                pltpu.VMEM(queries.shape, jnp.bfloat16),
                pltpu.VMEM(keys.shape, jnp.bfloat16),
                pltpu.VMEM(key_gain.shape, jnp.float32),
                pltpu.VMEM(key_bias.shape, jnp.float32),
                pltpu.VMEM(head_weights.shape[::-1], jnp.bfloat16),
                pltpu.VMEM(positions.shape, jnp.int32),
                pltpu.VMEM((1, DH), jnp.float32),
                pltpu.VMEM((heads * rows, DH), jnp.bfloat16),
                pltpu.VMEM((heads, rows, DH), jnp.float32),
                pltpu.VMEM((tokens, DH), jnp.bfloat16),
                pltpu.VMEM((n_chunk, n_head, rows_each, chunk), jnp.bfloat16),
                pltpu.VMEM((n_chunk, n_head - 1, rows_each, chunk), jnp.bfloat16),
                pltpu.SemaphoreType.DMA((7,)),
                pltpu.SemaphoreType.DMA((n_ctx,)),
                pltpu.SemaphoreType.DMA((n_ctx,)),
                pltpu.SemaphoreType.DMA((n_chunk, n_head - 1)),
                pltpu.SemaphoreType.DMA((n_chunk, n_head - 1)),
            ],
            compiler_params=pltpu.CompilerParams(
                collective_id=0, has_side_effects=True, vmem_limit_bytes=32 * 1024 * 1024
            ),
        )(*[pltpu.with_memory_space_constraint(x, pltpu.HBM) for x in operands])

    in_specs = (P("ctx", "head"), P("ctx", None), P(), P(), P("ctx", "head"), P("ctx"))
    out_specs = P(("ctx", "head"), None)
    return jax.shard_map(
        on_device, mesh=mesh, in_specs=in_specs, out_specs=out_specs, check_vma=False
    )
```

```python
import functools
import math

import jax
import jax.numpy as jnp
import numpy as np
from jax import lax
from jax.experimental import pallas as pl
from jax.experimental.pallas import tpu as pltpu
from jax.sharding import PartitionSpec as P

H = 64
DH = 128
ROPE = 64
MESH = pl.DeviceIdType.MESH


def yarn_frequencies(rope_dims):
    half_dims = rope_dims // 2
    exponent = np.arange(0, rope_dims, 2) / rope_dims
    extra_freq = 1.0 / 10000.0**exponent
    inter_freq = extra_freq / 40.0

    def correction(beta):
        return rope_dims * math.log(4096.0 / (beta * 2.0 * math.pi)) / (2.0 * math.log(10000.0))

    low_dim = max(math.floor(correction(32.0)), 0)
    high_dim = min(math.ceil(correction(1.0)), rope_dims - 1)
    ramp_values = np.clip((np.arange(half_dims) - low_dim) / (high_dim - low_dim), 0.0, 1.0)
    return (inter_freq * ramp_values + extra_freq * (1.0 - ramp_values)).astype(np.float32)


def sin_cos(angle):
    turns = jnp.floor(angle * (2.0 / math.pi) + 0.5)
    rest = angle - turns * 1.5703125
    rest = rest - turns * 4.837512969970703125e-4
    rest = rest - turns * 7.54978995489188216e-8
    square = rest * rest
    sine = ((-1.9515295891e-4 * square + 8.3321608736e-3) * square - 1.6666654611e-1) * (
        square * rest
    ) + rest
    cosine = (
        ((2.443315711809948e-5 * square - 1.388731625493765e-3) * square + 4.166664568298827e-2)
        * (square * square)
        - 0.5 * square
        + 1.0
    )
    quadrant = turns.astype(jnp.int32)
    odd = (quadrant & 1) == 1
    sine_out = jnp.where(odd, cosine, sine)
    cosine_out = jnp.where(odd, sine, cosine)
    sine_out = jnp.where((quadrant & 2) == 2, -sine_out, sine_out)
    cosine_out = jnp.where(((quadrant + 1) & 2) == 2, -cosine_out, cosine_out)
    return sine_out, cosine_out


def partner(index, bits):
    for b in range(bits.bit_length()):
        if bits >> b & 1:
            index = index + (1 - 2 * lax.rem(index // (1 << b), 2)) * (1 << b)
    return index


def kernel(
    n_ctx,
    n_head,
    chunk,
    queries_hbm,
    keys_hbm,
    gain_hbm,
    bias_hbm,
    weights_hbm,
    positions_hbm,
    freq_hbm,
    out_ref,
    q_in,
    k_in,
    gain_in,
    bias_in,
    w_in,
    pos_in,
    freq_in,
    w_flat,
    q_rot,
    w_wide,
    k_all,
    part_out,
    part_in,
    in_sem,
    key_send,
    key_recv,
    part_send,
    part_recv,
):
    c = lax.axis_index("ctx")
    g = lax.axis_index("head")
    rows = q_in.shape[0]
    heads = q_in.shape[1] // DH
    rows_each = rows // n_head
    tokens = n_ctx * rows
    first_end = 3 * tokens // 4
    late = c * rows >= first_end
    src_first = jnp.where(late, first_end // rows, 0)
    crossing = (c + 1) * rows > first_end
    dst_end = jnp.where(crossing, n_ctx, -(-first_end // rows))

    copies = [
        pltpu.make_async_copy(src, dst, in_sem.at[i])
        for i, (src, dst) in enumerate(
            [
                (positions_hbm, pos_in),
                (freq_hbm, freq_in),
                (keys_hbm, k_in),
                (gain_hbm, gain_in),
                (bias_hbm, bias_in),
                (weights_hbm, w_in),
                (queries_hbm, q_in),
            ]
        )
    ]
    for copy in copies[:5]:
        copy.start()

    barrier = pltpu.get_barrier_semaphore()

    def greet(i, carry):
        pl.semaphore_signal(barrier, inc=1, device_id={"ctx": i, "head": g}, device_id_type=MESH)
        return carry

    lax.fori_loop(src_first, c, greet, 0)
    for d in range(1, n_head):
        pl.semaphore_signal(
            barrier,
            inc=1,
            device_id={"ctx": c, "head": partner(g, d)},
            device_id_type=MESH,
        )

    for copy in copies[5:]:
        copy.start()
    out_ref[...] = jnp.zeros_like(out_ref)

    for copy in copies[:5]:
        copy.wait()
    pos_wide = jnp.broadcast_to(pos_in[...].reshape(1, rows).astype(jnp.float32), (rows, rows))
    here = lax.broadcasted_iota(jnp.int32, (rows, rows), 0)
    there = lax.broadcasted_iota(jnp.int32, (rows, rows), 1)
    pos = jnp.sum(jnp.where(here == there, pos_wide, 0.0), axis=1, keepdims=True)
    sine, cosine = sin_cos(pos * freq_in[...])
    lane = lax.broadcasted_iota(jnp.int32, (rows, DH), 1)
    half = ROPE // 2
    sine_low = jnp.where(lane < half, -sine, 0.0)
    sine_high = jnp.where((lane >= half) & (lane < ROPE), sine, 0.0)

    def rotate(values):
        return (
            values * cosine
            + pltpu.roll(values, DH - half, 1) * sine_low
            + pltpu.roll(values, half, 1) * sine_high
        )

    values = k_in[...].astype(jnp.float32)
    centered = values - jnp.mean(values, axis=-1, keepdims=True)
    spread = jnp.mean(centered * centered, axis=-1, keepdims=True)
    normed = centered * lax.rsqrt(spread + 1e-06) * gain_in[...].reshape(1, DH) + bias_in[
        ...
    ].reshape(1, DH)
    mine = pl.ds(pl.multiple_of(c * rows, rows), rows)
    k_all[mine, :] = rotate(normed).astype(jnp.bfloat16)

    pl.semaphore_wait(barrier, dst_end - c - 1 + n_head - 1)

    def key_copy(owner, target):
        place = pl.ds(pl.multiple_of(owner * rows, rows), rows)
        return pltpu.make_async_remote_copy(
            src_ref=k_all.at[place],
            dst_ref=k_all.at[place],
            send_sem=key_send.at[target],
            recv_sem=key_recv.at[owner],
            device_id={"ctx": target, "head": g},
            device_id_type=MESH,
        )

    def send_keys(i, carry):
        key_copy(c, dst_end + c - i).start()
        return carry

    lax.fori_loop(c + 1, dst_end, send_keys, 0)

    copies[5].wait()
    copies[6].wait()
    scale = 1.0 / math.sqrt(H * DH)
    w_flat[...] = w_in[...].astype(jnp.float32) * scale

    def prepare(step, carry):
        for j in range(4):
            h = step * 4 + j
            q_rot[pl.ds(pl.multiple_of(h * rows, rows), rows), :] = rotate(
                q_in[:, pl.ds(pl.multiple_of(h * DH, DH), DH)].astype(jnp.float32)
            ).astype(jnp.bfloat16)
            weight = jnp.where(here == there, w_flat[pl.ds(h, 1), :], 0.0)
            w_wide[h] = jnp.broadcast_to(jnp.sum(weight, axis=1, keepdims=True), (rows, DH))
        return carry

    lax.fori_loop(0, heads // 4, prepare, 0)

    row_glob = c * rows + lax.broadcasted_iota(jnp.int32, (rows, 1), 0)
    row_doc = row_glob - pos.astype(jnp.int32)
    per_chunk = chunk // rows
    chunk_first = src_first // per_chunk
    chunk_end = c // per_chunk + 1

    def part_copy(t, d):
        peer = partner(g, d)
        return pltpu.make_async_remote_copy(
            src_ref=part_out.at[t, peer],
            dst_ref=part_in.at[t, d - 1],
            send_sem=part_send.at[t, d - 1],
            recv_sem=part_recv.at[t, d - 1],
            device_id={"ctx": c, "head": peer},
            device_id_type=MESH,
        )

    def score(i, carry):
        t = chunk_end + chunk_first - 1 - i

        def arrive(i, carry):
            key_copy(i, c).wait_recv()
            return carry

        lax.fori_loop(
            jnp.maximum(src_first, t * per_chunk),
            jnp.minimum(c, (t + 1) * per_chunk),
            arrive,
            0,
        )
        first = pl.multiple_of(t * chunk, chunk)
        raw = lax.dot_general(
            q_rot[...],
            k_all[pl.ds(first, chunk), :],
            (((1,), (1,)), ((), ())),
            preferred_element_type=jnp.float32,
        )
        total = jnp.zeros((rows, chunk), jnp.float32)
        for h in range(heads):
            weight = w_wide[h]
            if chunk > DH:
                weight = jnp.concatenate([weight] * (chunk // DH), axis=1)
            total += jnp.maximum(raw[h * rows : (h + 1) * rows, :], 0.0) * weight
        key_glob = first + lax.broadcasted_iota(jnp.int32, (rows, chunk), 1)
        visible = (key_glob >= row_doc) & (key_glob <= row_glob)
        part = jnp.where(visible, total, 0.0).astype(jnp.bfloat16)
        for h in range(n_head):
            part_out[t, h] = part[h * rows_each : (h + 1) * rows_each, :]
        for d in range(n_head - 1, 0, -1):
            part_copy(t, d).start()
        return carry

    lax.fori_loop(chunk_first, chunk_end, score, 0)

    def gather(i, carry):
        t = chunk_end + chunk_first - 1 - i
        total = part_out[t, g].astype(jnp.float32)
        for d in range(1, n_head):
            part_copy(t, d).wait_recv()
            total += part_in[t, d - 1].astype(jnp.float32)
        out_ref[:, pl.ds(pl.multiple_of(t * chunk, chunk), chunk)] = total
        return carry

    lax.fori_loop(chunk_first, chunk_end, gather, 0)

    def sent_keys(i, carry):
        key_copy(c, i).wait_send()
        return carry

    lax.fori_loop(c + 1, dst_end, sent_keys, 0)

    def sent_parts(t, carry):
        for d in range(1, n_head):
            part_copy(t, d).wait_send()
        return carry

    lax.fori_loop(chunk_first, chunk_end, sent_parts, 0)


def solution(mesh):
    n_ctx, n_head = mesh.shape["ctx"], mesh.shape["head"]
    freqs = yarn_frequencies(ROPE)
    freq_wide = np.concatenate([freqs, freqs, np.zeros(DH - ROPE, np.float32)])[None, :]

    def on_device(queries, keys, key_gain, key_bias, head_weights, positions):
        rows = queries.shape[0]
        heads = queries.shape[1] // DH
        tokens = n_ctx * rows
        chunk = max(DH, tokens // 16)
        n_chunk = tokens // chunk
        rows_each = rows // n_head
        operands = (
            queries,
            keys,
            key_gain,
            key_bias,
            head_weights.T,
            positions,
            jnp.asarray(freq_wide),
        )
        return pl.pallas_call(
            functools.partial(kernel, n_ctx, n_head, chunk),
            out_shape=jax.ShapeDtypeStruct((rows_each, tokens), jnp.float32),
            in_specs=[pl.BlockSpec(memory_space=pltpu.HBM)] * 7,
            out_specs=pl.BlockSpec(memory_space=pltpu.VMEM),
            scratch_shapes=[
                pltpu.VMEM(queries.shape, jnp.bfloat16),
                pltpu.VMEM(keys.shape, jnp.bfloat16),
                pltpu.VMEM(key_gain.shape, jnp.float32),
                pltpu.VMEM(key_bias.shape, jnp.float32),
                pltpu.VMEM(head_weights.shape[::-1], jnp.bfloat16),
                pltpu.VMEM(positions.shape, jnp.int32),
                pltpu.VMEM((1, DH), jnp.float32),
                pltpu.VMEM((heads, rows), jnp.float32),
                pltpu.VMEM((heads * rows, DH), jnp.bfloat16),
                pltpu.VMEM((heads, rows, DH), jnp.float32),
                pltpu.VMEM((tokens, DH), jnp.bfloat16),
                pltpu.VMEM((n_chunk, n_head, rows_each, chunk), jnp.bfloat16),
                pltpu.VMEM((n_chunk, n_head - 1, rows_each, chunk), jnp.bfloat16),
                pltpu.SemaphoreType.DMA((7,)),
                pltpu.SemaphoreType.DMA((n_ctx,)),
                pltpu.SemaphoreType.DMA((n_ctx,)),
                pltpu.SemaphoreType.DMA((n_chunk, n_head - 1)),
                pltpu.SemaphoreType.DMA((n_chunk, n_head - 1)),
            ],
            compiler_params=pltpu.CompilerParams(
                collective_id=0, has_side_effects=True, vmem_limit_bytes=32 * 1024 * 1024
            ),
        )(*[pltpu.with_memory_space_constraint(x, pltpu.HBM) for x in operands])

    in_specs = (P("ctx", "head"), P("ctx", None), P(), P(), P("ctx", "head"), P("ctx"))
    out_specs = P(("ctx", "head"), None)
    return jax.shard_map(
        on_device, mesh=mesh, in_specs=in_specs, out_specs=out_specs, check_vma=False
    )
```

```python
import functools
import math

import jax
import jax.numpy as jnp
import numpy as np
from jax import lax
from jax.experimental import pallas as pl
from jax.experimental.pallas import tpu as pltpu
from jax.sharding import PartitionSpec as P

H = 64
DH = 128
ROPE = 64
MESH = pl.DeviceIdType.MESH


def yarn_frequencies(rope_dims):
    half_dims = rope_dims // 2
    exponent = np.arange(0, rope_dims, 2) / rope_dims
    extra_freq = 1.0 / 10000.0**exponent
    inter_freq = extra_freq / 40.0

    def correction(beta):
        return rope_dims * math.log(4096.0 / (beta * 2.0 * math.pi)) / (2.0 * math.log(10000.0))

    low_dim = max(math.floor(correction(32.0)), 0)
    high_dim = min(math.ceil(correction(1.0)), rope_dims - 1)
    ramp_values = np.clip((np.arange(half_dims) - low_dim) / (high_dim - low_dim), 0.0, 1.0)
    return (inter_freq * ramp_values + extra_freq * (1.0 - ramp_values)).astype(np.float32)


def sin_cos(angle):
    turns = jnp.floor(angle * (2.0 / math.pi) + 0.5)
    rest = angle - turns * 1.5703125
    rest = rest - turns * 4.837512969970703125e-4
    rest = rest - turns * 7.54978995489188216e-8
    square = rest * rest
    sine = ((-1.9515295891e-4 * square + 8.3321608736e-3) * square - 1.6666654611e-1) * (
        square * rest
    ) + rest
    cosine = (
        ((2.443315711809948e-5 * square - 1.388731625493765e-3) * square + 4.166664568298827e-2)
        * (square * square)
        - 0.5 * square
        + 1.0
    )
    quadrant = turns.astype(jnp.int32)
    odd = (quadrant & 1) == 1
    sine_out = jnp.where(odd, cosine, sine)
    cosine_out = jnp.where(odd, sine, cosine)
    sine_out = jnp.where((quadrant & 2) == 2, -sine_out, sine_out)
    cosine_out = jnp.where(((quadrant + 1) & 2) == 2, -cosine_out, cosine_out)
    return sine_out, cosine_out


def partner(index, bits):
    for b in range(bits.bit_length()):
        if bits >> b & 1:
            index = index + (1 - 2 * lax.rem(index // (1 << b), 2)) * (1 << b)
    return index


def kernel(
    n_ctx,
    n_head,
    chunk,
    queries_hbm,
    keys_hbm,
    gain_hbm,
    bias_hbm,
    weights_hbm,
    positions_hbm,
    freq_hbm,
    out_ref,
    q_in,
    k_in,
    gain_in,
    bias_in,
    w_in,
    pos_in,
    freq_in,
    w_flat,
    q_rot,
    w_wide,
    k_all,
    part_out,
    part_in,
    in_sem,
    key_send,
    key_recv,
    part_send,
    part_recv,
):
    c = lax.axis_index("ctx")
    g = lax.axis_index("head")
    rows = q_in.shape[0]
    heads = q_in.shape[1] // DH
    rows_each = rows // n_head
    tokens = n_ctx * rows
    first_end = 3 * tokens // 4
    late = c * rows >= first_end
    src_first = jnp.where(late, first_end // rows, 0)
    crossing = (c + 1) * rows > first_end
    dst_end = jnp.where(crossing, n_ctx, -(-first_end // rows))

    copies = [
        pltpu.make_async_copy(src, dst, in_sem.at[i])
        for i, (src, dst) in enumerate(
            [
                (positions_hbm, pos_in),
                (freq_hbm, freq_in),
                (keys_hbm, k_in),
                (gain_hbm, gain_in),
                (bias_hbm, bias_in),
                (weights_hbm, w_in),
                (queries_hbm, q_in),
            ]
        )
    ]
    for copy in copies[:5]:
        copy.start()

    barrier = pltpu.get_barrier_semaphore()

    def greet(i, carry):
        pl.semaphore_signal(barrier, inc=1, device_id={"ctx": i, "head": g}, device_id_type=MESH)
        return carry

    lax.fori_loop(src_first, c, greet, 0)
    for d in range(1, n_head):
        pl.semaphore_signal(
            barrier,
            inc=1,
            device_id={"ctx": c, "head": partner(g, d)},
            device_id_type=MESH,
        )

    for copy in copies[5:]:
        copy.start()
    out_ref[...] = jnp.zeros_like(out_ref)

    for copy in copies[:5]:
        copy.wait()
    pos_wide = jnp.broadcast_to(pos_in[...].reshape(1, rows).astype(jnp.float32), (rows, rows))
    here = lax.broadcasted_iota(jnp.int32, (rows, rows), 0)
    there = lax.broadcasted_iota(jnp.int32, (rows, rows), 1)
    pos = jnp.sum(jnp.where(here == there, pos_wide, 0.0), axis=1, keepdims=True)
    sine, cosine = sin_cos(pos * freq_in[...])
    lane = lax.broadcasted_iota(jnp.int32, (rows, DH), 1)
    half = ROPE // 2
    sine_low = jnp.where(lane < half, -sine, 0.0)
    sine_high = jnp.where((lane >= half) & (lane < ROPE), sine, 0.0)

    def rotate(values):
        return (
            values * cosine
            + pltpu.roll(values, DH - half, 1) * sine_low
            + pltpu.roll(values, half, 1) * sine_high
        )

    values = k_in[...].astype(jnp.float32)
    centered = values - jnp.mean(values, axis=-1, keepdims=True)
    spread = jnp.mean(centered * centered, axis=-1, keepdims=True)
    normed = centered * lax.rsqrt(spread + 1e-06) * gain_in[...].reshape(1, DH) + bias_in[
        ...
    ].reshape(1, DH)
    mine = pl.ds(pl.multiple_of(c * rows, rows), rows)
    k_all[mine, :] = rotate(normed).astype(jnp.bfloat16)

    pl.semaphore_wait(barrier, dst_end - c - 1 + n_head - 1)

    def key_copy(owner, target):
        place = pl.ds(pl.multiple_of(owner * rows, rows), rows)
        return pltpu.make_async_remote_copy(
            src_ref=k_all.at[place],
            dst_ref=k_all.at[place],
            send_sem=key_send.at[target],
            recv_sem=key_recv.at[owner],
            device_id={"ctx": target, "head": g},
            device_id_type=MESH,
        )

    def send_keys(i, carry):
        key_copy(c, jnp.where(i + 1 < dst_end, i + 1, c + 1)).start()
        return carry

    lax.fori_loop(c + 1, dst_end, send_keys, 0)

    copies[5].wait()
    copies[6].wait()
    scale = 1.0 / math.sqrt(H * DH)
    w_flat[...] = w_in[...].astype(jnp.float32) * scale

    unroll = math.gcd(heads, 8)

    def prepare(step, carry):
        for j in range(unroll):
            h = step * unroll + j
            q_rot[pl.ds(pl.multiple_of(h * rows, rows), rows), :] = rotate(
                q_in[:, pl.ds(pl.multiple_of(h * DH, DH), DH)].astype(jnp.float32)
            ).astype(jnp.bfloat16)
            weight = jnp.where(here == there, w_flat[pl.ds(h, 1), :], 0.0)
            w_wide[h] = jnp.broadcast_to(jnp.sum(weight, axis=1, keepdims=True), (rows, DH))
        return carry

    lax.fori_loop(0, heads // unroll, prepare, 0)

    row_glob = c * rows + lax.broadcasted_iota(jnp.int32, (rows, 1), 0)
    row_doc = row_glob - pos.astype(jnp.int32)
    per_chunk = chunk // rows
    chunk_first = src_first // per_chunk
    chunk_end = c // per_chunk + 1

    def part_copy(t, d):
        peer = partner(g, d)
        return pltpu.make_async_remote_copy(
            src_ref=part_out.at[t, peer],
            dst_ref=part_in.at[t, d - 1],
            send_sem=part_send.at[t, d - 1],
            recv_sem=part_recv.at[t, d - 1],
            device_id={"ctx": c, "head": peer},
            device_id_type=MESH,
        )

    def score(i, carry):
        t = chunk_end + chunk_first - 1 - i

        def arrive(i, carry):
            key_copy(i, c).wait_recv()
            return carry

        lax.fori_loop(
            jnp.maximum(src_first, t * per_chunk),
            jnp.minimum(c, (t + 1) * per_chunk),
            arrive,
            0,
        )
        first = pl.multiple_of(t * chunk, chunk)
        raw = lax.dot_general(
            q_rot[...],
            k_all[pl.ds(first, chunk), :],
            (((1,), (1,)), ((), ())),
            preferred_element_type=jnp.float32,
        )
        total = jnp.zeros((rows, chunk), jnp.float32)
        for h in range(heads):
            weight = w_wide[h]
            if chunk > DH:
                weight = jnp.concatenate([weight] * (chunk // DH), axis=1)
            total += jnp.maximum(raw[h * rows : (h + 1) * rows, :], 0.0) * weight
        key_glob = first + lax.broadcasted_iota(jnp.int32, (rows, chunk), 1)
        visible = (key_glob >= row_doc) & (key_glob <= row_glob)
        part = jnp.where(visible, total, 0.0).astype(jnp.bfloat16)
        for h in range(n_head):
            part_out[t, h] = part[h * rows_each : (h + 1) * rows_each, :]
        for d in range(n_head - 1, 0, -1):
            part_copy(t, d).start()
        return carry

    lax.fori_loop(chunk_first, chunk_end, score, 0)

    def gather(i, carry):
        t = chunk_end + chunk_first - 1 - i
        total = part_out[t, g].astype(jnp.float32)
        for d in range(1, n_head):
            part_copy(t, d).wait_recv()
            total += part_in[t, d - 1].astype(jnp.float32)
        out_ref[:, pl.ds(pl.multiple_of(t * chunk, chunk), chunk)] = total
        return carry

    lax.fori_loop(chunk_first, chunk_end, gather, 0)

    def sent_keys(i, carry):
        key_copy(c, i).wait_send()
        return carry

    lax.fori_loop(c + 1, dst_end, sent_keys, 0)

    def sent_parts(t, carry):
        for d in range(1, n_head):
            part_copy(t, d).wait_send()
        return carry

    lax.fori_loop(chunk_first, chunk_end, sent_parts, 0)


def solution(mesh):
    n_ctx, n_head = mesh.shape["ctx"], mesh.shape["head"]
    freqs = yarn_frequencies(ROPE)
    freq_wide = np.concatenate([freqs, freqs, np.zeros(DH - ROPE, np.float32)])[None, :]

    def on_device(queries, keys, key_gain, key_bias, head_weights, positions):
        rows = queries.shape[0]
        heads = queries.shape[1] // DH
        tokens = n_ctx * rows
        chunk = max(DH, tokens // 16)
        n_chunk = tokens // chunk
        rows_each = rows // n_head
        operands = (
            queries,
            keys,
            key_gain,
            key_bias,
            head_weights.T,
            positions,
            jnp.asarray(freq_wide),
        )
        return pl.pallas_call(
            functools.partial(kernel, n_ctx, n_head, chunk),
            out_shape=jax.ShapeDtypeStruct((rows_each, tokens), jnp.float32),
            in_specs=[pl.BlockSpec(memory_space=pltpu.HBM)] * 7,
            out_specs=pl.BlockSpec(memory_space=pltpu.VMEM),
            scratch_shapes=[
                pltpu.VMEM(queries.shape, jnp.bfloat16),
                pltpu.VMEM(keys.shape, jnp.bfloat16),
                pltpu.VMEM(key_gain.shape, jnp.float32),
                pltpu.VMEM(key_bias.shape, jnp.float32),
                pltpu.VMEM(head_weights.shape[::-1], jnp.bfloat16),
                pltpu.VMEM(positions.shape, jnp.int32),
                pltpu.VMEM((1, DH), jnp.float32),
                pltpu.VMEM((heads, rows), jnp.float32),
                pltpu.VMEM((heads * rows, DH), jnp.bfloat16),
                pltpu.VMEM((heads, rows, DH), jnp.float32),
                pltpu.VMEM((tokens, DH), jnp.bfloat16),
                pltpu.VMEM((n_chunk, n_head, rows_each, chunk), jnp.bfloat16),
                pltpu.VMEM((n_chunk, n_head - 1, rows_each, chunk), jnp.bfloat16),
                pltpu.SemaphoreType.DMA((7,)),
                pltpu.SemaphoreType.DMA((n_ctx,)),
                pltpu.SemaphoreType.DMA((n_ctx,)),
                pltpu.SemaphoreType.DMA((n_chunk, n_head - 1)),
                pltpu.SemaphoreType.DMA((n_chunk, n_head - 1)),
            ],
            compiler_params=pltpu.CompilerParams(
                collective_id=0, has_side_effects=True, vmem_limit_bytes=32 * 1024 * 1024
            ),
        )(*[pltpu.with_memory_space_constraint(x, pltpu.HBM) for x in operands])

    in_specs = (P("ctx", "head"), P("ctx", None), P(), P(), P("ctx", "head"), P("ctx"))
    out_specs = P(("ctx", "head"), None)
    return jax.shard_map(
        on_device, mesh=mesh, in_specs=in_specs, out_specs=out_specs, check_vma=False
    )
```

```python
import functools
import math

import jax
import jax.numpy as jnp
import numpy as np
from jax import lax
from jax.experimental import pallas as pl
from jax.experimental.pallas import tpu as pltpu
from jax.sharding import PartitionSpec as P

H = 64
DH = 128
ROPE = 64
MESH = pl.DeviceIdType.MESH


def yarn_frequencies(rope_dims):
    half_dims = rope_dims // 2
    exponent = np.arange(0, rope_dims, 2) / rope_dims
    extra_freq = 1.0 / 10000.0**exponent
    inter_freq = extra_freq / 40.0

    def correction(beta):
        return rope_dims * math.log(4096.0 / (beta * 2.0 * math.pi)) / (2.0 * math.log(10000.0))

    low_dim = max(math.floor(correction(32.0)), 0)
    high_dim = min(math.ceil(correction(1.0)), rope_dims - 1)
    ramp_values = np.clip((np.arange(half_dims) - low_dim) / (high_dim - low_dim), 0.0, 1.0)
    return (inter_freq * ramp_values + extra_freq * (1.0 - ramp_values)).astype(np.float32)


def sin_cos(angle):
    turns = jnp.floor(angle * (2.0 / math.pi) + 0.5)
    rest = angle - turns * 1.5703125
    rest = rest - turns * 4.837512969970703125e-4
    rest = rest - turns * 7.54978995489188216e-8
    square = rest * rest
    sine = ((-1.9515295891e-4 * square + 8.3321608736e-3) * square - 1.6666654611e-1) * (
        square * rest
    ) + rest
    cosine = (
        ((2.443315711809948e-5 * square - 1.388731625493765e-3) * square + 4.166664568298827e-2)
        * (square * square)
        - 0.5 * square
        + 1.0
    )
    quadrant = turns.astype(jnp.int32)
    odd = (quadrant & 1) == 1
    sine_out = jnp.where(odd, cosine, sine)
    cosine_out = jnp.where(odd, sine, cosine)
    sine_out = jnp.where((quadrant & 2) == 2, -sine_out, sine_out)
    cosine_out = jnp.where(((quadrant + 1) & 2) == 2, -cosine_out, cosine_out)
    return sine_out, cosine_out


def partner(index, bits):
    for b in range(bits.bit_length()):
        if bits >> b & 1:
            index = index + (1 - 2 * lax.rem(index // (1 << b), 2)) * (1 << b)
    return index


def kernel(
    n_ctx,
    n_head,
    chunk,
    queries_hbm,
    keys_hbm,
    gain_hbm,
    bias_hbm,
    weights_hbm,
    positions_hbm,
    freq_hbm,
    out_ref,
    q_in,
    k_in,
    gain_in,
    bias_in,
    w_in,
    pos_in,
    freq_in,
    w_flat,
    q_rot,
    w_wide,
    k_all,
    part_out,
    part_in,
    in_sem,
    key_send,
    key_recv,
    part_send,
    part_recv,
):
    c = lax.axis_index("ctx")
    g = lax.axis_index("head")
    rows = q_in.shape[0]
    heads = q_in.shape[1] // DH
    rows_each = rows // n_head
    tokens = n_ctx * rows
    first_end = 3 * tokens // 4
    late = c * rows >= first_end
    src_first = jnp.where(late, first_end // rows, 0)
    crossing = (c + 1) * rows > first_end
    dst_end = jnp.where(crossing, n_ctx, -(-first_end // rows))

    copies = [
        pltpu.make_async_copy(src, dst, in_sem.at[i])
        for i, (src, dst) in enumerate(
            [
                (positions_hbm, pos_in),
                (freq_hbm, freq_in),
                (keys_hbm, k_in),
                (gain_hbm, gain_in),
                (bias_hbm, bias_in),
                (weights_hbm, w_in),
                (queries_hbm, q_in),
            ]
        )
    ]
    for copy in copies[:5]:
        copy.start()

    barrier = pltpu.get_barrier_semaphore()

    def greet(i, carry):
        pl.semaphore_signal(barrier, inc=1, device_id={"ctx": i, "head": g}, device_id_type=MESH)
        return carry

    lax.fori_loop(src_first, c, greet, 0)
    for d in range(1, n_head):
        pl.semaphore_signal(
            barrier,
            inc=1,
            device_id={"ctx": c, "head": partner(g, d)},
            device_id_type=MESH,
        )

    for copy in copies[5:]:
        copy.start()
    out_ref[...] = jnp.zeros_like(out_ref)

    for copy in copies[:5]:
        copy.wait()
    pos_wide = jnp.broadcast_to(pos_in[...].reshape(1, rows).astype(jnp.float32), (rows, rows))
    here = lax.broadcasted_iota(jnp.int32, (rows, rows), 0)
    there = lax.broadcasted_iota(jnp.int32, (rows, rows), 1)
    pos = jnp.sum(jnp.where(here == there, pos_wide, 0.0), axis=1, keepdims=True)
    sine, cosine = sin_cos(pos * freq_in[...])
    lane = lax.broadcasted_iota(jnp.int32, (rows, DH), 1)
    half = ROPE // 2
    sine_low = jnp.where(lane < half, -sine, 0.0)
    sine_high = jnp.where((lane >= half) & (lane < ROPE), sine, 0.0)

    def rotate(values):
        return (
            values * cosine
            + pltpu.roll(values, DH - half, 1) * sine_low
            + pltpu.roll(values, half, 1) * sine_high
        )

    values = k_in[...].astype(jnp.float32)
    centered = values - jnp.mean(values, axis=-1, keepdims=True)
    spread = jnp.mean(centered * centered, axis=-1, keepdims=True)
    normed = centered * lax.rsqrt(spread + 1e-06) * gain_in[...].reshape(1, DH) + bias_in[
        ...
    ].reshape(1, DH)
    mine = pl.ds(pl.multiple_of(c * rows, rows), rows)
    k_all[mine, :] = rotate(normed).astype(jnp.bfloat16)

    pl.semaphore_wait(barrier, dst_end - c - 1 + n_head - 1)

    def key_copy(owner, target):
        place = pl.ds(pl.multiple_of(owner * rows, rows), rows)
        return pltpu.make_async_remote_copy(
            src_ref=k_all.at[place],
            dst_ref=k_all.at[place],
            send_sem=key_send.at[target],
            recv_sem=key_recv.at[owner],
            device_id={"ctx": target, "head": g},
            device_id_type=MESH,
        )

    def send_keys(i, carry):
        key_copy(c, i).start()
        return carry

    lax.fori_loop(c + 1, dst_end, send_keys, 0)

    copies[5].wait()
    copies[6].wait()
    scale = 1.0 / math.sqrt(H * DH)
    w_flat[...] = w_in[...].astype(jnp.float32) * scale

    unroll = math.gcd(heads, 8)

    def prepare(step, carry):
        for j in range(unroll):
            h = step * unroll + j
            q_rot[pl.ds(pl.multiple_of(h * rows, rows), rows), :] = rotate(
                q_in[:, pl.ds(pl.multiple_of(h * DH, DH), DH)].astype(jnp.float32)
            ).astype(jnp.bfloat16)
            weight = jnp.where(here == there, w_flat[pl.ds(h, 1), :], 0.0)
            w_wide[h] = jnp.broadcast_to(jnp.sum(weight, axis=1, keepdims=True), (rows, DH))
        return carry

    lax.fori_loop(0, heads // unroll, prepare, 0)

    row_glob = c * rows + lax.broadcasted_iota(jnp.int32, (rows, 1), 0)
    row_doc = row_glob - pos.astype(jnp.int32)
    per_chunk = chunk // rows
    chunk_first = src_first // per_chunk
    chunk_end = c // per_chunk + 1

    def part_copy(t, d):
        peer = partner(g, d)
        return pltpu.make_async_remote_copy(
            src_ref=part_out.at[t, peer],
            dst_ref=part_in.at[t, d - 1],
            send_sem=part_send.at[t, d - 1],
            recv_sem=part_recv.at[t, d - 1],
            device_id={"ctx": c, "head": peer},
            device_id_type=MESH,
        )

    def score(i, carry):
        t = chunk_end + chunk_first - 1 - i

        def arrive(i, carry):
            key_copy(i, c).wait_recv()
            return carry

        lax.fori_loop(
            jnp.maximum(src_first, t * per_chunk),
            jnp.minimum(c, (t + 1) * per_chunk),
            arrive,
            0,
        )
        first = pl.multiple_of(t * chunk, chunk)
        raw = lax.dot_general(
            q_rot[...],
            k_all[pl.ds(first, chunk), :],
            (((1,), (1,)), ((), ())),
            preferred_element_type=jnp.float32,
        )
        total = jnp.zeros((rows, chunk), jnp.float32)
        for h in range(heads):
            weight = w_wide[h]
            if chunk > DH:
                weight = jnp.concatenate([weight] * (chunk // DH), axis=1)
            total += jnp.maximum(raw[h * rows : (h + 1) * rows, :], 0.0) * weight
        key_glob = first + lax.broadcasted_iota(jnp.int32, (rows, chunk), 1)
        visible = (key_glob >= row_doc) & (key_glob <= row_glob)
        part = jnp.where(visible, total, 0.0).astype(jnp.bfloat16)
        for h in range(n_head):
            part_out[t, h] = part[h * rows_each : (h + 1) * rows_each, :]
        for d in range(n_head - 1, 0, -1):
            part_copy(t, d).start()
        return carry

    lax.fori_loop(chunk_first, chunk_end, score, 0)

    def gather(i, carry):
        t = chunk_end + chunk_first - 1 - i
        total = part_out[t, g].astype(jnp.float32)
        for d in range(1, n_head):
            part_copy(t, d).wait_recv()
            total += part_in[t, d - 1].astype(jnp.float32)
        out_ref[:, pl.ds(pl.multiple_of(t * chunk, chunk), chunk)] = total
        return carry

    lax.fori_loop(chunk_first, chunk_end, gather, 0)

    def sent_keys(i, carry):
        key_copy(c, i).wait_send()
        return carry

    lax.fori_loop(c + 1, dst_end, sent_keys, 0)

    def sent_parts(t, carry):
        for d in range(1, n_head):
            part_copy(t, d).wait_send()
        return carry

    lax.fori_loop(chunk_first, chunk_end, sent_parts, 0)


def solution(mesh):
    n_ctx, n_head = mesh.shape["ctx"], mesh.shape["head"]
    freqs = yarn_frequencies(ROPE)
    freq_wide = np.concatenate([freqs, freqs, np.zeros(DH - ROPE, np.float32)])[None, :]

    def on_device(queries, keys, key_gain, key_bias, head_weights, positions):
        rows = queries.shape[0]
        heads = queries.shape[1] // DH
        tokens = n_ctx * rows
        chunk = max(DH, tokens // 16)
        n_chunk = tokens // chunk
        rows_each = rows // n_head
        operands = (
            queries,
            keys,
            key_gain,
            key_bias,
            head_weights.T,
            positions,
            jnp.asarray(freq_wide),
        )
        return pl.pallas_call(
            functools.partial(kernel, n_ctx, n_head, chunk),
            out_shape=jax.ShapeDtypeStruct((rows_each, tokens), jnp.float32),
            in_specs=[pl.BlockSpec(memory_space=pltpu.HBM)] * 7,
            out_specs=pl.BlockSpec(memory_space=pltpu.VMEM),
            scratch_shapes=[
                pltpu.VMEM(queries.shape, jnp.bfloat16),
                pltpu.VMEM(keys.shape, jnp.bfloat16),
                pltpu.VMEM(key_gain.shape, jnp.float32),
                pltpu.VMEM(key_bias.shape, jnp.float32),
                pltpu.VMEM(head_weights.shape[::-1], jnp.bfloat16),
                pltpu.VMEM(positions.shape, jnp.int32),
                pltpu.VMEM((1, DH), jnp.float32),
                pltpu.VMEM((heads, rows), jnp.float32),
                pltpu.VMEM((heads * rows, DH), jnp.bfloat16),
                pltpu.VMEM((heads, rows, DH), jnp.float32),
                pltpu.VMEM((tokens, DH), jnp.bfloat16),
                pltpu.VMEM((n_chunk, n_head, rows_each, chunk), jnp.bfloat16),
                pltpu.VMEM((n_chunk, n_head - 1, rows_each, chunk), jnp.bfloat16),
                pltpu.SemaphoreType.DMA((7,)),
                pltpu.SemaphoreType.DMA((n_ctx,)),
                pltpu.SemaphoreType.DMA((n_ctx,)),
                pltpu.SemaphoreType.DMA((n_chunk, n_head - 1)),
                pltpu.SemaphoreType.DMA((n_chunk, n_head - 1)),
            ],
            compiler_params=pltpu.CompilerParams(
                collective_id=0, has_side_effects=True, vmem_limit_bytes=32 * 1024 * 1024
            ),
        )(*[pltpu.with_memory_space_constraint(x, pltpu.HBM) for x in operands])

    in_specs = (P("ctx", "head"), P("ctx", None), P(), P(), P("ctx", "head"), P("ctx"))
    out_specs = P(("ctx", "head"), None)
    return jax.shard_map(
        on_device, mesh=mesh, in_specs=in_specs, out_specs=out_specs, check_vma=False
    )
```
